32 devices in a mesh: dp: 8 (over z, x), tensor: 4 (over y, core).
Axes of the slice: x: 2, y: 2, z: 4, core: 2. Of those that a mesh axis runs over, the one named last changes fastest.
Arguments:
- gradient: bfloat16 [8, 512, 16384], P(None, 'dp', 'tensor')
- second_moment: bfloat16 [8, 512, 16384], P(None, 'dp', 'tensor'), may hold values from 0.049804688 to 2
- slot_of_block: int32 [4, 64], P('tensor'), may hold values from 0 to 127, as said below
- stats_left: float32 [4, 128, 512, 512], P('tensor', 'dp'), as said below
- stats_right: float32 [4, 128, 512, 512], P('tensor', 'dp'), as said below
- root_left: bfloat16 [4, 128, 512, 512], P('tensor', 'dp'), as said below
- root_right: bfloat16 [4, 128, 512, 512], P('tensor', 'dp'), as said below
Outputs:
- update: bfloat16 [8, 512, 16384], P(None, 'dp', 'tensor')
- second_moment_new: bfloat16 [8, 512, 16384], P(None, 'dp', 'tensor')
- stats_left_new: float32 [4, 128, 512, 512], P('tensor', 'dp')
- stats_right_new: float32 [4, 128, 512, 512], P('tensor', 'dp')
The draws below stay inside these ranges and needn't reach their ends.
Inputs may be any that keep to these rules, and one draw needn't show every extreme that they name: `slot_of_block`: the entries of one row are distinct; slot s belongs to owner s // 16 of dp; in every row some owner holds 16 blocks. `stats_left`: symmetric matrices. `stats_right`: symmetric matrices. `root_left`: symmetric matrices. `root_right`: symmetric matrices.
All inputs are finite; a program needn't handle non-finite values.
Results may differ from the reference program's by a relative error of at most 0.0064.
Values may be sent and summed in bfloat16 or wider, within the bound.
A program may use at most 256 MiB of HBM per device.

```python
import math
import jax
import jax.numpy as jnp
from jax import lax

B = 512
DW = 4096
FW = 16384
RB = 8
NCB = 8
NBC = 64
CAP = 16
N_DP = 8
N_TENSOR = 4


def draw_gradient(key, part):
    key = jax.random.fold_in(key, 11)
    key_rows = jax.random.fold_in(key, 0)
    key_cols = jax.random.fold_in(key, 1)
    key_noise = jax.random.fold_in(key, 2)
    key_group = jax.random.fold_in(key, 4)
    row_scale = jnp.exp(jax.random.uniform(key_rows, (RB, B, 1), jnp.float32, 0.0, math.log(4.0)))
    col_scale = jnp.exp(jax.random.uniform(key_cols, (1, 1, FW), jnp.float32, 0.0, math.log(4.0)))
    position = (jnp.arange(B) // (B // N_DP)).astype(jnp.float32)
    ramp = jnp.sqrt(1.0 + 2.0 * position / max(N_DP - 1, 1)).reshape(1, B, 1)
    group = jnp.arange(FW) // (FW // N_TENSOR)
    group_ramp = jnp.sqrt(1.0 + 2.0 * group.astype(jnp.float32) / max(N_TENSOR - 1, 1))
    group_gain = jnp.exp(jax.random.uniform(key_group, (N_TENSOR,), jnp.float32, -0.4, 0.4))
    randoms = jax.random.normal(key_noise, (RB, B, FW), jnp.float32)
    group_scale = (group_ramp * group_gain[group]).reshape(1, 1, FW)
    return (randoms * row_scale * col_scale * group_scale * ramp).astype(jnp.bfloat16)


def symmetric(key, diag_lo, diag_hi, spread):
    key_noise, key_diag = jax.random.split(key)
    randoms = jax.random.normal(key_noise, (N_TENSOR, N_DP * CAP, B, B), jnp.float32)
    diagonal = jnp.exp(jax.random.uniform(key_diag, (N_TENSOR, N_DP * CAP, B, 1), jnp.float32, math.log(diag_lo), math.log(diag_hi)))
    identity = jnp.eye(B, dtype=jnp.float32)
    return spread / math.sqrt(B) * 0.5 * (randoms + jnp.swapaxes(randoms, 2, 3)) + identity * diagonal


def draw_stats_left(key, part):
    key = jax.random.fold_in(key, 21)
    return symmetric(key, 0.5, 2.0, 0.5)


def draw_stats_right(key, part):
    key = jax.random.fold_in(key, 22)
    return symmetric(key, 0.5, 2.0, 0.5)


def draw_root_left(key, part):
    key = jax.random.fold_in(key, 23)
    return symmetric(key, 1.0, 2.0, 0.5).astype(jnp.bfloat16)


def draw_root_right(key, part):
    key = jax.random.fold_in(key, 24)
    return symmetric(key, 1.0, 2.0, 0.5).astype(jnp.bfloat16)


def draw_slot_of_block(key, part):
    key = jax.random.fold_in(key, 31)

    def one_row(row_key):
        key_owner, key_rank, key_order = jax.random.split(row_key, 3)
        total_slots = N_DP * CAP
        full_owner = jax.random.randint(key_owner, (), 0, N_DP)
        ranking = jax.random.permutation(key_rank, total_slots)
        numbers = jnp.arange(total_slots)
        scores = jnp.where(numbers // CAP == full_owner, numbers - total_slots, ranking)
        chosen = jnp.argsort(scores, stable=True)[:NBC]
        return jax.random.permutation(key_order, chosen).astype(jnp.int32)
    return jax.vmap(one_row)(jax.random.split(key, N_TENSOR))


def shard_levels(key, extent, pieces, least, largest):
    factor_of = 1.0
    for axis_at, blocks in pieces:
        steps = jax.random.uniform(jax.random.fold_in(jax.random.fold_in(key, 6), axis_at), (blocks,), jnp.float32, least / len(pieces), largest / len(pieces))
        factor_of = factor_of * jnp.repeat(jnp.exp(steps), extent[axis_at] // blocks).reshape((-1,) + (1,) * (len(extent) - 1 - axis_at))
    return factor_of


def setup_inputs(seed: int = 0) -> dict:
    arg_keys = jax.random.split(jax.random.key(seed), 8)
    return {
        "gradient": draw_gradient(jax.random.fold_in(arg_keys[7], 71), 0),
        "second_moment": jnp.clip(jnp.exp(math.log(2.0) - 3.6927934 * jax.random.uniform(arg_keys[1], (RB, B, FW), jnp.float32) ** shard_levels(arg_keys[1], (RB, B, FW), ((1, 8), (2, 4)), -0.2, 0.2)), 0.049804688, 2.0).astype(jnp.bfloat16),
        "slot_of_block": draw_slot_of_block(jax.random.fold_in(arg_keys[7], 71), 0),
        "stats_left": draw_stats_left(jax.random.fold_in(arg_keys[7], 71), 0),
        "stats_right": draw_stats_right(jax.random.fold_in(arg_keys[7], 71), 0),
        "root_left": draw_root_left(jax.random.fold_in(arg_keys[7], 71), 0),
        "root_right": draw_root_right(jax.random.fold_in(arg_keys[7], 71), 0),
    }


clip_level = 0.5
decay_moment = 0.95
decay_stats = 0.9
eps_adam = 1e-08
eps_graft = 1e-06

def reference(gradient, second_moment, slot_of_block, stats_left, stats_right, root_left, root_right):
    grad_wide = gradient.astype(jnp.float32)
    total_square = jnp.sum(grad_wide * grad_wide)
    clip_factor = clip_level * math.sqrt(DW * FW) / jnp.sqrt(total_square)
    clipped = clip_factor * grad_wide
    moment = decay_moment * second_moment.astype(jnp.float32) + (1.0 - decay_moment) * clipped * clipped
    adam_step = clipped / (jnp.sqrt(moment) + eps_adam)
    moment_new = moment.astype(jnp.bfloat16)
    squares = (adam_step * adam_step).reshape(RB, B, N_TENSOR, NCB, B)
    adam_norm = jnp.transpose(lax.optimization_barrier(jnp.sum(squares, axis=(1, 4))), (1, 0, 2)).reshape(N_TENSOR * NBC)
    grad_blocks = jnp.transpose(gradient.reshape(RB, B, N_TENSOR, NCB, B), (2, 0, 3, 1, 4)).reshape(N_TENSOR * NBC, B, B)
    table = slot_of_block.reshape(N_TENSOR * NBC)
    area = float(B * B)

    def step_block(index, carry):
        left_new, right_new, updates = carry
        column = index // NBC
        slot = table[index]
        grad_block = grad_blocks[index]
        gram_left = lax.dot_general(grad_block, grad_block, (((1,), (1,)), ((), ())), preferred_element_type=jnp.float32)
        gram_right = lax.dot_general(grad_block, grad_block, (((0,), (0,)), ((), ())), preferred_element_type=jnp.float32)
        square_clip = clip_factor * clip_factor
        left_block = decay_stats * stats_left[column, slot] + (1.0 - decay_stats) * square_clip * gram_left
        right_block = decay_stats * stats_right[column, slot] + (1.0 - decay_stats) * square_clip * gram_right
        scaled = (clip_factor * grad_block.astype(jnp.float32)).astype(jnp.bfloat16)
        applied = jnp.dot(root_left[column, slot], scaled, preferred_element_type=jnp.float32).astype(jnp.bfloat16)
        precond = jnp.dot(applied, root_right[column, slot], preferred_element_type=jnp.float32).astype(jnp.bfloat16)
        precond_wide = precond.astype(jnp.float32)
        ratio = jnp.sqrt(adam_norm[index] / area / (jnp.sum(precond_wide * precond_wide) / area + eps_graft))
        update_block = (ratio * precond_wide).astype(jnp.bfloat16)
        left_new = left_new.at[column, slot].set(left_block)
        right_new = right_new.at[column, slot].set(right_block)
        updates = updates.at[index].set(update_block)
        return (left_new, right_new, updates)
    start = (stats_left, stats_right, jnp.zeros((N_TENSOR * NBC, B, B), jnp.bfloat16))
    left_new, right_new, updates = lax.fori_loop(0, N_TENSOR * NBC, step_block, start)
    update = jnp.transpose(updates.reshape(N_TENSOR, RB, NCB, B, B), (1, 3, 0, 2, 4)).reshape(RB, B, FW)
    return (update, moment_new, left_new, right_new)
```

```python
import functools
import math

import jax
import jax.numpy as jnp
from jax import lax
from jax.experimental import pallas as pl
from jax.experimental.pallas import tpu as pltpu
from jax.sharding import PartitionSpec as P

clip_level = 0.5
decay_moment = 0.95
decay_stats = 0.9
eps_adam = 1e-08
eps_graft = 1e-06
vmem_bytes = 48 * 1024 * 1024


def params():
    return pltpu.CompilerParams(vmem_limit_bytes=vmem_bytes)


def pack_kernel(col_blocks, block_size, count, blocks_ref, grad_ref, out_ref):
    owner = pl.program_id(0)
    for at in range(count):
        block = blocks_ref[owner * count + at]
        row = block // col_blocks
        column = pl.multiple_of((block % col_blocks) * block_size, block_size)
        out_ref[0, at] = grad_ref[row, :, pl.ds(column, block_size)]


def pack(blocks, gradient, owners, block_size):
    count = blocks.shape[0] // owners
    row_blocks, piece_rows, columns = gradient.shape
    return pl.pallas_call(
        functools.partial(pack_kernel, columns // block_size, block_size, count),
        grid_spec=pltpu.PrefetchScalarGridSpec(
            num_scalar_prefetch=1,
            grid=(owners,),
            in_specs=[pl.BlockSpec((row_blocks, piece_rows, columns), lambda o, b: (0, 0, 0))],
            out_specs=pl.BlockSpec((1, count, piece_rows, block_size), lambda o, b: (o, 0, 0, 0)),
        ),
        out_shape=jax.ShapeDtypeStruct((owners, count, piece_rows, block_size), jnp.bfloat16),
        compiler_params=params(),
        name="pack",
    )(blocks, gradient)


def slot_kernel(
    slots_ref, active_ref, clip_ref, grad_ref, left_ref, right_ref, root_left_ref, root_right_ref,
    left_out, right_out, precond_out, norm_out,
):
    at = pl.program_id(0)
    owners, _, piece_rows, block_size = grad_ref.shape

    @pl.when(active_ref[at] != 0)
    def _():
        clip = clip_ref[0]
        factor = (1.0 - decay_stats) * (clip * clip)
        block = grad_ref[...].reshape(block_size, block_size)
        gram_left = lax.dot_general(
            block, block, (((1,), (1,)), ((), ())), preferred_element_type=jnp.float32
        )
        left_out[0, 0] = decay_stats * left_ref[0, 0] + factor * gram_left
        gram_right = lax.dot_general(
            block, block, (((0,), (0,)), ((), ())), preferred_element_type=jnp.float32
        )
        right_out[0, 0] = decay_stats * right_ref[0, 0] + factor * gram_right
        scaled = (clip * block.astype(jnp.float32)).astype(jnp.bfloat16)
        applied = jnp.dot(
            root_left_ref[0, 0], scaled, preferred_element_type=jnp.float32
        ).astype(jnp.bfloat16)
        precond = jnp.dot(
            applied, root_right_ref[0, 0], preferred_element_type=jnp.float32
        ).astype(jnp.bfloat16)
        precond_out[...] = precond.reshape(owners, 1, piece_rows, block_size)
        wide = precond.astype(jnp.float32)
        norm_out[0] = jnp.sum(wide * wide, axis=0, keepdims=True)

    @pl.when(active_ref[at] == 0)
    def _():
        left_out[0, 0] = left_ref[0, 0]
        right_out[0, 0] = right_ref[0, 0]
        precond_out[...] = jnp.zeros_like(precond_out)
        norm_out[...] = jnp.zeros_like(norm_out)


def process_slots(slots, active, clip, arrived, stats_left, stats_right, root_left, root_right):
    owners, capacity, piece_rows, block_size = arrived.shape
    square = pl.BlockSpec((1, 1, block_size, block_size), lambda j, s, a, c: (0, s[j], 0, 0))
    pieces = pl.BlockSpec((owners, 1, piece_rows, block_size), lambda j, s, a, c: (0, j, 0, 0))
    return pl.pallas_call(
        slot_kernel,
        grid_spec=pltpu.PrefetchScalarGridSpec(
            num_scalar_prefetch=3,
            grid=(capacity,),
            in_specs=[pieces, square, square, square, square],
            out_specs=[
                square,
                square,
                pieces,
                pl.BlockSpec((1, 1, block_size), lambda j, s, a, c: (j, 0, 0)),
            ],
        ),
        out_shape=[
            jax.ShapeDtypeStruct(stats_left.shape, jnp.float32),
            jax.ShapeDtypeStruct(stats_right.shape, jnp.float32),
            jax.ShapeDtypeStruct(arrived.shape, jnp.bfloat16),
            jax.ShapeDtypeStruct((capacity, 1, block_size), jnp.float32),
        ],
        compiler_params=params(),
        name="slots",
    )(slots, active, clip, arrived, stats_left, stats_right, root_left, root_right)


def moment_kernel(clip_ref, grad_ref, moment_ref, moment_out, norm_out):
    clipped = clip_ref[0] * grad_ref[0].astype(jnp.float32)
    moment = (
        decay_moment * moment_ref[0].astype(jnp.float32) + (1.0 - decay_moment) * clipped * clipped
    )
    moment_out[0] = moment.astype(jnp.bfloat16)
    adam_step = clipped / (jnp.sqrt(moment) + eps_adam)
    norm_out[0] = jnp.sum(adam_step * adam_step, axis=0, keepdims=True)


def update_moment(clip, gradient, second_moment):
    row_blocks, piece_rows, columns = gradient.shape
    rows = pl.BlockSpec((1, piece_rows, columns), lambda i, c: (i, 0, 0))
    size = gradient.size
    return pl.pallas_call(
        moment_kernel,
        grid_spec=pltpu.PrefetchScalarGridSpec(
            num_scalar_prefetch=1,
            grid=(row_blocks,),
            in_specs=[rows, rows],
            out_specs=[rows, pl.BlockSpec((1, 1, columns), lambda i, c: (i, 0, 0))],
        ),
        out_shape=[
            jax.ShapeDtypeStruct(gradient.shape, jnp.bfloat16),
            jax.ShapeDtypeStruct((row_blocks, 1, columns), jnp.float32),
        ],
        compiler_params=params(),
        cost_estimate=pl.CostEstimate(
            flops=12 * size, bytes_accessed=6 * size, transcendentals=2 * size
        ),
        name="moment",
    )(clip, gradient, second_moment)


def unpack_kernel(col_blocks, places_ref, ratio_ref, *refs):
    out_ref = refs[-1]
    row = pl.program_id(0)
    block_size = out_ref.shape[2] // col_blocks
    for column in range(col_blocks):
        ratio = ratio_ref[row * col_blocks + column]
        wide = refs[column][0, 0].astype(jnp.float32)
        out_ref[0, :, column * block_size : (column + 1) * block_size] = (ratio * wide).astype(
            jnp.bfloat16
        )


def unpack(places, ratio, returned, shape):
    owners, count, piece_rows, block_size = returned.shape
    row_blocks, _, columns = shape
    col_blocks = columns // block_size

    def piece(column):
        def index(i, places, ratio):
            place = places[i * col_blocks + column]
            return (place // count, place % count, 0, 0)

        return pl.BlockSpec((1, 1, piece_rows, block_size), index)

    return pl.pallas_call(
        functools.partial(unpack_kernel, col_blocks),
        grid_spec=pltpu.PrefetchScalarGridSpec(
            num_scalar_prefetch=2,
            grid=(row_blocks,),
            in_specs=[piece(column) for column in range(col_blocks)],
            out_specs=pl.BlockSpec((1, piece_rows, columns), lambda i, p, r: (i, 0, 0)),
        ),
        out_shape=jax.ShapeDtypeStruct(shape, jnp.bfloat16),
        compiler_params=params(),
        name="unpack",
    )(places, ratio, *([returned] * col_blocks))


def per_device(
    gradient, second_moment, slot_of_block, stats_left, stats_right, root_left, root_right
):
    owners = lax.axis_size("dp")
    my_owner = lax.axis_index("dp")
    row_blocks, piece_rows, columns = gradient.shape
    block_size = piece_rows * owners
    col_blocks = columns // block_size
    block_count = row_blocks * col_blocks
    capacity = stats_left.shape[1]
    all_rows = row_blocks * block_size
    all_columns = columns * lax.axis_size("tensor")
    area = float(block_size * block_size)

    table = slot_of_block[0]
    numbers = jnp.arange(block_count, dtype=jnp.int32)
    owner = table // capacity
    ahead = (owner[None, :] == owner[:, None]) & (table[None, :] < table[:, None])
    places = owner * capacity + jnp.sum(ahead, axis=1, dtype=jnp.int32)
    all_places = jnp.arange(owners * capacity, dtype=jnp.int32)
    blocks = jnp.sum(
        jnp.where(places[None, :] == all_places[:, None], numbers[None, :], 0),
        axis=1,
        dtype=jnp.int32,
    )
    local = jnp.arange(capacity, dtype=jnp.int32)
    used = jnp.any(table[None, :] == (my_owner * capacity + local)[:, None], axis=1)
    before = local[None, :] < local[:, None]
    used_count = jnp.sum(used, dtype=jnp.int32)
    order = jnp.where(
        used,
        jnp.sum(before & used[None, :], axis=1, dtype=jnp.int32),
        used_count + jnp.sum(before & ~used[None, :], axis=1, dtype=jnp.int32),
    )
    slots = jnp.sum(
        jnp.where(order[None, :] == local[:, None], local[None, :], 0), axis=1, dtype=jnp.int32
    )
    active = (local < used_count).astype(jnp.int32)

    outgoing = pack(blocks, gradient, owners, block_size)
    arrived = lax.all_to_all(outgoing, "dp", split_axis=0, concat_axis=0, tiled=True)

    grad_wide = gradient.astype(jnp.float32)
    total_square = lax.psum(jnp.sum(grad_wide * grad_wide), ("dp", "tensor"))
    clip_factor = clip_level * math.sqrt(all_rows * all_columns) / jnp.sqrt(total_square)
    clip = clip_factor.reshape(1)

    left_new, right_new, precond, norms = process_slots(
        slots, active, clip, arrived, stats_left, stats_right, root_left, root_right
    )
    returned = lax.all_to_all(precond, "dp", split_axis=0, concat_axis=0, tiled=True)

    later_clip, norms = lax.optimization_barrier((clip, norms))
    moment_new, adam_rows = update_moment(later_clip, gradient, second_moment)
    adam_part = jnp.sum(
        adam_rows.reshape(row_blocks, col_blocks, block_size), axis=2
    ).reshape(block_count)
    owned = places[:, None] == (my_owner * capacity + local)[None, :]
    precond_part = jnp.sum(
        jnp.where(owned, jnp.sum(norms, axis=(1, 2))[None, :], 0.0), axis=1
    )
    adam_total, precond_total = lax.psum((adam_part, precond_part), "dp")
    ratio = jnp.sqrt(adam_total / area / (precond_total / area + eps_graft))
    update = unpack(places, ratio, returned, gradient.shape)
    return update, moment_new, left_new, right_new


def solution(mesh):
    placed = (
        P(None, "dp", "tensor"),
        P(None, "dp", "tensor"),
        P("tensor", None),
        P("tensor", "dp", None, None),
        P("tensor", "dp", None, None),
        P("tensor", "dp", None, None),
        P("tensor", "dp", None, None),
    )
    return jax.shard_map(
        per_device,
        mesh=mesh,
        in_specs=placed,
        out_specs=(
            P(None, "dp", "tensor"),
            P(None, "dp", "tensor"),
            P("tensor", "dp", None, None),
            P("tensor", "dp", None, None),
        ),
        check_vma=False,
    )
```

```python
import functools
import math

import jax
import jax.numpy as jnp
from jax import lax
from jax.experimental import pallas as pl
from jax.experimental.pallas import tpu as pltpu
from jax.sharding import PartitionSpec as P

clip_level = 0.5
decay_moment = 0.95
decay_stats = 0.9
eps_adam = 1e-08
eps_graft = 1e-06
vmem_bytes = 60 * 1024 * 1024


def params():
    return pltpu.CompilerParams(vmem_limit_bytes=vmem_bytes)


def pack_kernel(col_blocks, block_size, count, blocks_ref, grad_ref, out_ref):
    owner = pl.program_id(0)
    for at in range(count):
        block = blocks_ref[owner * count + at]
        row = block // col_blocks
        column = pl.multiple_of((block % col_blocks) * block_size, block_size)
        out_ref[0, at] = grad_ref[row, :, pl.ds(column, block_size)]


def pack(blocks, gradient, owners, block_size):
    count = blocks.shape[0] // owners
    row_blocks, piece_rows, columns = gradient.shape
    return pl.pallas_call(
        functools.partial(pack_kernel, columns // block_size, block_size, count),
        grid_spec=pltpu.PrefetchScalarGridSpec(
            num_scalar_prefetch=1,
            grid=(owners,),
            in_specs=[pl.BlockSpec((row_blocks, piece_rows, columns), lambda o, b: (0, 0, 0))],
            out_specs=pl.BlockSpec((1, count, piece_rows, block_size), lambda o, b: (o, 0, 0, 0)),
        ),
        out_shape=jax.ShapeDtypeStruct((owners, count, piece_rows, block_size), jnp.bfloat16),
        compiler_params=params(),
        name="pack",
    )(blocks, gradient)


def slot_kernel(
    slots_ref, active_ref, clip_ref, grad_ref, left_ref, right_ref, root_left_ref, root_right_ref,
    *refs,
):
    left_out, right_out, precond_out, norm_out = refs[-4:]
    at = pl.program_id(0)
    owners, _, piece_rows, block_size = grad_ref.shape

    @pl.when(active_ref[at] != 0)
    def _():
        clip = clip_ref[0]
        factor = (1.0 - decay_stats) * (clip * clip)
        block = grad_ref[...].reshape(block_size, block_size)
        gram_left = lax.dot_general(
            block, block, (((1,), (1,)), ((), ())), preferred_element_type=jnp.float32
        )
        left_out[0, 0] = decay_stats * left_ref[0, 0] + factor * gram_left
        gram_right = lax.dot_general(
            block, block, (((0,), (0,)), ((), ())), preferred_element_type=jnp.float32
        )
        right_out[0, 0] = decay_stats * right_ref[0, 0] + factor * gram_right
        scaled = (clip * block.astype(jnp.float32)).astype(jnp.bfloat16)
        applied = jnp.dot(
            root_left_ref[0, 0], scaled, preferred_element_type=jnp.float32
        ).astype(jnp.bfloat16)
        precond = jnp.dot(
            applied, root_right_ref[0, 0], preferred_element_type=jnp.float32
        ).astype(jnp.bfloat16)
        precond_out[...] = precond.reshape(owners, 1, piece_rows, block_size)
        wide = precond.astype(jnp.float32)
        norm_out[0] = jnp.sum(wide * wide, axis=0, keepdims=True)

    @pl.when(active_ref[at] == 0)
    def _():
        left_out[0, 0] = left_ref[0, 0]
        right_out[0, 0] = right_ref[0, 0]
        precond_out[...] = jnp.zeros_like(precond_out)
        norm_out[...] = jnp.zeros_like(norm_out)


def process_slots(
    slots, active, clip, arrived, stats_left, stats_right, root_left, root_right, earlier
):
    owners, count, piece_rows, block_size = arrived.shape
    square = pl.BlockSpec((1, 1, block_size, block_size), lambda j, s, a, c: (0, s[j], 0, 0))
    pieces = pl.BlockSpec((owners, 1, piece_rows, block_size), lambda j, s, a, c: (0, j, 0, 0))
    entries = block_size * block_size
    return pl.pallas_call(
        slot_kernel,
        grid_spec=pltpu.PrefetchScalarGridSpec(
            num_scalar_prefetch=3,
            grid=(count,),
            in_specs=[pieces, square, square, square, square]
            + [pl.BlockSpec(memory_space=pl.ANY)] * len(earlier),
            out_specs=[
                square,
                square,
                pieces,
                pl.BlockSpec((1, 1, block_size), lambda j, s, a, c: (j, 0, 0)),
            ],
        ),
        out_shape=[
            jax.ShapeDtypeStruct(stats_left.shape, jnp.float32),
            jax.ShapeDtypeStruct(stats_right.shape, jnp.float32),
            jax.ShapeDtypeStruct(arrived.shape, jnp.bfloat16),
            jax.ShapeDtypeStruct((count, 1, block_size), jnp.float32),
        ],
        input_output_aliases={8 + at: at for at in range(len(earlier))},
        compiler_params=params(),
        cost_estimate=pl.CostEstimate(
            flops=8 * count * entries * block_size,
            bytes_accessed=24 * count * entries,
            transcendentals=0,
        ),
        name="slots",
    )(slots, active, clip, arrived, stats_left, stats_right, root_left, root_right, *earlier)


def moment_kernel(clip_ref, grad_ref, moment_ref, moment_out, norm_out):
    clipped = clip_ref[0] * grad_ref[0].astype(jnp.float32)
    moment = (
        decay_moment * moment_ref[0].astype(jnp.float32) + (1.0 - decay_moment) * clipped * clipped
    )
    moment_out[0] = moment.astype(jnp.bfloat16)
    adam_step = clipped / (jnp.sqrt(moment) + eps_adam)
    norm_out[0] = jnp.sum(adam_step * adam_step, axis=0, keepdims=True)


def update_moment(clip, gradient, second_moment):
    row_blocks, piece_rows, columns = gradient.shape
    rows = pl.BlockSpec((1, piece_rows, columns), lambda i, c: (i, 0, 0))
    size = gradient.size
    return pl.pallas_call(
        moment_kernel,
        grid_spec=pltpu.PrefetchScalarGridSpec(
            num_scalar_prefetch=1,
            grid=(row_blocks,),
            in_specs=[rows, rows],
            out_specs=[rows, pl.BlockSpec((1, 1, columns), lambda i, c: (i, 0, 0))],
        ),
        out_shape=[
            jax.ShapeDtypeStruct(gradient.shape, jnp.bfloat16),
            jax.ShapeDtypeStruct((row_blocks, 1, columns), jnp.float32),
        ],
        compiler_params=params(),
        cost_estimate=pl.CostEstimate(
            flops=12 * size, bytes_accessed=6 * size, transcendentals=2 * size
        ),
        name="moment",
    )(clip, gradient, second_moment)


def unpack_kernel(col_blocks, count, parts, places_ref, ratio_ref, *refs):
    out_ref = refs[-1]
    row = pl.program_id(0)
    block_size = out_ref.shape[2] // col_blocks
    for column in range(col_blocks):
        number = row * col_blocks + column
        ratio = ratio_ref[number]
        part = (places_ref[number] % (parts * count)) // count
        for at in range(parts):

            @pl.when(part == at)
            def _(column=column, at=at, ratio=ratio):
                wide = refs[column * parts + at][0, 0].astype(jnp.float32)
                out_ref[0, :, column * block_size : (column + 1) * block_size] = (
                    ratio * wide
                ).astype(jnp.bfloat16)


def unpack(places, ratio, returned, shape):
    parts = len(returned)
    owners, count, piece_rows, block_size = returned[0].shape
    row_blocks, _, columns = shape
    col_blocks = columns // block_size

    def piece(column, at):
        def index(i, places, ratio):
            place = places[i * col_blocks + column]
            rank = place % (parts * count)
            here = (rank // count == at).astype(jnp.int32)
            return (here * (place // (parts * count)), here * (rank % count), 0, 0)

        return pl.BlockSpec((1, 1, piece_rows, block_size), index)

    return pl.pallas_call(
        functools.partial(unpack_kernel, col_blocks, count, parts),
        grid_spec=pltpu.PrefetchScalarGridSpec(
            num_scalar_prefetch=2,
            grid=(row_blocks,),
            in_specs=[piece(column, at) for column in range(col_blocks) for at in range(parts)],
            out_specs=pl.BlockSpec((1, piece_rows, columns), lambda i, p, r: (i, 0, 0)),
        ),
        out_shape=jax.ShapeDtypeStruct(shape, jnp.bfloat16),
        compiler_params=params(),
        name="unpack",
    )(places, ratio, *(list(returned) * col_blocks))


def per_device(
    gradient, second_moment, slot_of_block, stats_left, stats_right, root_left, root_right
):
    owners = lax.axis_size("dp")
    my_owner = lax.axis_index("dp")
    row_blocks, piece_rows, columns = gradient.shape
    block_size = piece_rows * owners
    col_blocks = columns // block_size
    block_count = row_blocks * col_blocks
    capacity = stats_left.shape[1]
    all_rows = row_blocks * block_size
    all_columns = columns * lax.axis_size("tensor")
    area = float(block_size * block_size)

    table = slot_of_block[0]
    numbers = jnp.arange(block_count, dtype=jnp.int32)
    owner = table // capacity
    ahead = (owner[None, :] == owner[:, None]) & (table[None, :] < table[:, None])
    places = owner * capacity + jnp.sum(ahead, axis=1, dtype=jnp.int32)
    all_places = jnp.arange(owners * capacity, dtype=jnp.int32)
    blocks = jnp.sum(
        jnp.where(places[None, :] == all_places[:, None], numbers[None, :], 0),
        axis=1,
        dtype=jnp.int32,
    )
    local = jnp.arange(capacity, dtype=jnp.int32)
    used = jnp.any(table[None, :] == (my_owner * capacity + local)[:, None], axis=1)
    before = local[None, :] < local[:, None]
    used_count = jnp.sum(used, dtype=jnp.int32)
    order = jnp.where(
        used,
        jnp.sum(before & used[None, :], axis=1, dtype=jnp.int32),
        used_count + jnp.sum(before & ~used[None, :], axis=1, dtype=jnp.int32),
    )
    slots = jnp.sum(
        jnp.where(order[None, :] == local[:, None], local[None, :], 0), axis=1, dtype=jnp.int32
    )
    active = (local < used_count).astype(jnp.int32)

    parts = 2 if capacity % 2 == 0 else 1
    count = capacity // parts
    by_owner = blocks.reshape(owners, capacity)

    def packed(part):
        chosen = by_owner[:, part * count : (part + 1) * count].reshape(owners * count)
        return pack(chosen, gradient, owners, block_size)

    def exchange(pieces):
        return lax.all_to_all(pieces, "dp", split_axis=0, concat_axis=0, tiled=True)

    outgoing = [packed(part) for part in range(parts)]
    arrived = [exchange(outgoing[0])]

    grad_wide = gradient.astype(jnp.float32)
    my_square = jnp.sum(grad_wide * grad_wide)
    *later, my_square = lax.optimization_barrier((*outgoing[1:], my_square))
    total_square = lax.psum(my_square, ("dp", "tensor"))
    *later, total_square = lax.optimization_barrier((*later, total_square))
    arrived.extend(exchange(pieces) for pieces in later)
    clip_factor = clip_level * math.sqrt(all_rows * all_columns) / jnp.sqrt(total_square)
    clip = clip_factor.reshape(1)

    earlier, returned, norms = (), [], []
    for part in range(parts):
        chosen = slice(part * count, (part + 1) * count)
        left_new, right_new, precond, norm = process_slots(
            slots[chosen], active[chosen], clip, arrived[part],
            stats_left, stats_right, root_left, root_right, earlier,
        )
        earlier = (left_new, right_new)
        if returned:
            precond, returned[-1] = lax.optimization_barrier((precond, returned[-1]))
        returned.append(exchange(precond))
        norms.append(norm)
    norms = jnp.concatenate(norms)

    moment_new, adam_rows = update_moment(clip, gradient, second_moment)
    adam_part = jnp.sum(
        adam_rows.reshape(row_blocks, col_blocks, block_size), axis=2
    ).reshape(block_count)
    owned = places[:, None] == (my_owner * capacity + local)[None, :]
    precond_part = jnp.sum(
        jnp.where(owned, jnp.sum(norms, axis=(1, 2))[None, :], 0.0), axis=1
    )
    adam_total, precond_total = lax.psum((adam_part, precond_part), "dp")
    ratio = jnp.sqrt(adam_total / area / (precond_total / area + eps_graft))
    update = unpack(places, ratio, returned, gradient.shape)
    return update, moment_new, left_new, right_new


def solution(mesh):
    placed = (
        P(None, "dp", "tensor"),
        P(None, "dp", "tensor"),
        P("tensor", None),
        P("tensor", "dp", None, None),
        P("tensor", "dp", None, None),
        P("tensor", "dp", None, None),
        P("tensor", "dp", None, None),
    )
    return jax.shard_map(
        per_device,
        mesh=mesh,
        in_specs=placed,
        out_specs=(
            P(None, "dp", "tensor"),
            P(None, "dp", "tensor"),
            P("tensor", "dp", None, None),
            P("tensor", "dp", None, None),
        ),
        check_vma=False,
    )
```
